1024 devices in a mesh: dp: 128 (over z_hi, y, x, core), mp: 8 (over z_lo).
Axes of the slice: x: 4, y: 8, z: 16 (z_hi: 2, z_lo: 8; z = z_hi * 8 + z_lo), core: 2. Of those that a mesh axis runs over, the one named last changes fastest.
Arguments:
- queries: bfloat16 [32768, 3072], P('dp', 'mp'), may hold values from -6 to 6
- keys: bfloat16 [32768, 3072], P('dp', 'mp'), may hold values from -6 to 6
- values: bfloat16 [32768, 3072], P('dp', 'mp'), may hold values from -24 to 24
- w_out: bfloat16 [3072, 6144], P(None, ('mp', 'dp')), may hold values from -0.109375 to 0.109375
- cotangent: bfloat16 [32768, 6144], P('dp', 'mp'), may hold values from -6 to 6
Outputs:
- branch_out: bfloat16 [32768, 6144], P('dp', 'mp')
- grad_queries: bfloat16 [32768, 3072], P('dp', 'mp')
- grad_keys: bfloat16 [32768, 3072], P('dp', 'mp')
- grad_values: bfloat16 [32768, 3072], P('dp', 'mp')
The draws below stay inside these ranges and needn't reach their ends.
All inputs are finite; a program needn't handle non-finite values.
Results may differ from the reference program's by a relative error of at most 0.03.
Values may be sent and summed in bfloat16 or wider, within the bound.
No kernel may reach another device: no remote copies, remote signals or barrier semaphores. Data moves between devices by JAX's collectives and lax.ppermute only.
A program may use at most 64 MiB of HBM per device.

```python
import math
import jax
import jax.numpy as jnp
from jax import lax

D = 6144
HD = 128
SEQ = 256
HEADS_DEV = 3
TOKENS = 32768
FOUT = 3072
N_MP = 8


def draw_queries(key, part):
    key = jax.random.fold_in(key, 11)
    entry_key = jax.random.fold_in(key, 0)
    entries = jnp.clip(jax.random.normal(entry_key, (TOKENS, FOUT), jnp.float32), -6.0, 6.0)
    return entries.astype(jnp.bfloat16)


def draw_keys(key, part):
    key = jax.random.fold_in(key, 23)
    entries = jnp.clip(jax.random.normal(key, (TOKENS, FOUT), jnp.float32), -6.0, 6.0)
    return entries.astype(jnp.bfloat16)


def shard_levels(key, shape, cuts, low, top_value):
    factor_of, own = 1.0, jax.random.fold_in(key, 6)
    for dim, parts in cuts:
        heights = jnp.exp(jax.random.uniform(jax.random.fold_in(own, dim), (parts,), jnp.float32, low / len(cuts), top_value / len(cuts)))
        factor_of = factor_of * jnp.repeat(heights, shape[dim] // parts).reshape([-1 if axis == dim else 1 for axis in range(len(shape))])
    return factor_of


def gaussian(own_key, shape, spread, limit, pieces=(), held_as=jnp.bfloat16):
    values = jax.random.normal(own_key, shape, jnp.float32) * spread
    if len(pieces) > 0:
        values = shard_levels(own_key, shape, pieces, -0.22, 0.18) * values
    return jnp.clip(values, min=-limit, max=limit).astype(held_as)


def setup_inputs(seed: int = 0) -> dict:
    key_list = jax.random.split(jax.random.key(seed), 6)
    return {
        "queries": draw_queries(jax.random.fold_in(key_list[5], 71), 0),
        "keys": draw_keys(jax.random.fold_in(key_list[5], 71), 0),
        "values": gaussian(key_list[2], (TOKENS, FOUT), 4.0, 24.0, ((0, 128), (1, 8))),
        "w_out": gaussian(key_list[3], (FOUT, D), FOUT ** -0.5, 0.109375, ((1, 1024),)),
        "cotangent": gaussian(key_list[4], (TOKENS, D), 1.0, 6.0, ((0, 128), (1, 8))),
    }


def reference(queries, keys, values, w_out, cotangent):
    head_count = HEADS_DEV * N_MP
    group_width = HEADS_DEV * HD
    feature_group = D // N_MP
    score_scale = 1.0 / math.sqrt(HD)
    w_groups = w_out.reshape(N_MP, group_width, D).astype(jnp.float32)
    w_split = w_out.reshape(FOUT, N_MP, feature_group).astype(jnp.float32)

    def one_image(inputs_one):
        query_img, key_img, value_img, cot_img = inputs_one
        query_heads = query_img.reshape(SEQ, head_count, HD).astype(jnp.float32)
        key_heads = key_img.reshape(SEQ, head_count, HD).astype(jnp.float32)
        value_heads = value_img.reshape(SEQ, head_count, HD).astype(jnp.float32)
        scores = jnp.einsum('qhd,khd->hqk', query_heads, key_heads) * score_scale
        softmax_out = jax.nn.softmax(scores, -1)
        softmax_low = softmax_out.astype(jnp.bfloat16)
        head_out = jnp.einsum('hqk,khd->qhd', softmax_low.astype(jnp.float32), value_heads).astype(jnp.bfloat16)
        pieces_out = jnp.einsum('tjc,jcd->tjd', head_out.reshape(SEQ, N_MP, group_width).astype(jnp.float32), w_groups).astype(jnp.bfloat16)
        pieces_out = lax.optimization_barrier(pieces_out)
        branch_img = lax.optimization_barrier(jnp.sum(pieces_out.astype(jnp.float32), 1)).astype(jnp.bfloat16)
        pieces_grad = jnp.einsum('tjd,fjd->tjf', cot_img.reshape(SEQ, N_MP, feature_group).astype(jnp.float32), w_split).astype(jnp.bfloat16)
        pieces_grad = lax.optimization_barrier(pieces_grad)
        grad_out = lax.optimization_barrier(jnp.sum(pieces_grad.astype(jnp.float32), 1)).astype(jnp.bfloat16)
        grad_heads = grad_out.reshape(SEQ, head_count, HD).astype(jnp.float32)
        soft_grad = jnp.einsum('qhd,khd->hqk', grad_heads, value_heads)
        score_grad = (softmax_out * (soft_grad - lax.optimization_barrier(jnp.sum(soft_grad * softmax_out, -1, keepdims=True)))).astype(jnp.bfloat16)
        score_wide = score_grad.astype(jnp.float32)
        grad_query = (jnp.einsum('hqk,khd->qhd', score_wide, key_heads) * score_scale).astype(jnp.bfloat16)
        grad_key = (jnp.einsum('hqk,qhd->khd', score_wide, query_heads) * score_scale).astype(jnp.bfloat16)
        grad_value = jnp.einsum('hqk,qhd->khd', softmax_low.astype(jnp.float32), grad_heads).astype(jnp.bfloat16)
        return (branch_img, grad_query.reshape(SEQ, FOUT), grad_key.reshape(SEQ, FOUT), grad_value.reshape(SEQ, FOUT))
    branch, grad_q, grad_k, grad_v = lax.map(one_image, (queries.reshape(-1, SEQ, FOUT), keys.reshape(-1, SEQ, FOUT), values.reshape(-1, SEQ, FOUT), cotangent.reshape(-1, SEQ, D)))
    return (branch.reshape(TOKENS, D), grad_q.reshape(TOKENS, FOUT), grad_k.reshape(TOKENS, FOUT), grad_v.reshape(TOKENS, FOUT))
```

```python
import math

import jax
import jax.numpy as jnp
import numpy as np
from jax import lax
from jax.sharding import Mesh, PartitionSpec as P

HD = 128
SEQ = 256
SIZES = (2, 8, 4, 2, 8)
DP = ("zh", "y", "x", "core")
CZ = ("core", "zl")
BF16 = jnp.bfloat16
F32 = jnp.float32


def shift(block, axis, by):
    n = lax.axis_size(axis)
    return lax.ppermute(block, axis, [(i, (i + by) % n) for i in range(n)])


def ring_gather(block, axis):
    n = lax.axis_size(axis)
    up = down = block
    blocks = [block]
    for step in range(1, n // 2 + 1):
        up = shift(up, axis, 1)
        blocks.append(up)
        if 2 * step < n:
            down = shift(down, axis, -1)
            blocks.append(down)
    return blocks


def ring_offsets(n):
    offsets = [0]
    for step in range(1, n // 2 + 1):
        offsets.append(-step)
        if 2 * step < n:
            offsets.append(step)
    return np.array(offsets)


def feature_of_row(rows_dev):
    nz, ny, nx, nc = (lax.axis_size(a) for a in DP)
    yo, xo = ring_offsets(ny), ring_offsets(nx)
    grid = np.indices((ny, nx, 2, nc, rows_dev)).reshape(5, -1)
    y = (lax.axis_index("y") + jnp.asarray(yo[grid[0]] + ny)) % ny
    x = (lax.axis_index("x") + jnp.asarray(xo[grid[1]] + nx)) % nx
    z = (lax.axis_index("zh") + jnp.asarray(grid[2])) % nz
    return (((z * ny + y) * nx + x) * nc + jnp.asarray(grid[3])) * rows_dev + jnp.asarray(
        grid[4]
    )


def by_core(own, other):
    first = lax.axis_index("core") == 0
    return jnp.where(first, own, other), jnp.where(first, other, own)


def gather_projection(w_out, groups):
    rows_dev = w_out.shape[1]
    width = w_out.shape[0] // groups
    core = lax.axis_index("core")
    shard = w_out.T.reshape(rows_dev, groups, width).transpose(1, 0, 2)
    half = groups // 2
    mine = lax.dynamic_slice_in_dim(shard, core * half, half, 0)
    theirs = lax.dynamic_slice_in_dim(shard, (1 - core) * half, half, 0)
    z_own = shift(mine, "zh", 1)
    nz = lax.axis_size("zh")
    nc = lax.axis_size("core")
    z_cross = lax.ppermute(
        theirs,
        ("zh", "core"),
        [(z * nc + c, ((z + 1) % nz) * nc + 1 - c) for z in range(nz) for c in range(nc)],
    )
    cross = shift(theirs, "core", 1)
    base = jnp.concatenate([*by_core(mine, cross), *by_core(z_own, z_cross)], 1)
    quarter = half // 2
    ny, nx = lax.axis_size("y"), lax.axis_size("x")
    rows = base.shape[1]
    first = jnp.concatenate(ring_gather(base[:quarter], "x"), 1)
    second = jnp.concatenate(ring_gather(base[quarter:], "y"), 1)
    first = jnp.concatenate(ring_gather(first, "y"), 1)
    second = jnp.stack(ring_gather(second, "x"), 1)
    second = (
        second.reshape(quarter, nx, ny, rows, width)
        .transpose(0, 2, 1, 3, 4)
        .reshape(quarter, nx * ny * rows, width)
    )
    first_pair = by_core(first, shift(first, "core", 1))
    second_pair = by_core(second, shift(second, "core", 1))
    return jnp.concatenate([first_pair[0], second_pair[0], first_pair[1], second_pair[1]], 0)


def on_device(queries, keys, values, w_out, cotangent):
    row_count = queries.shape[0]
    group_width = queries.shape[1]
    local_heads = group_width // HD
    n = lax.axis_size("zl")
    me = lax.axis_index("zl")
    core = lax.axis_index("core")
    features = cotangent.shape[1]
    score_scale = 1.0 / math.sqrt(HD)
    heads = (row_count, local_heads, HD)
    query_heads = queries.reshape(heads)
    key_heads = keys.reshape(heads)
    value_heads = values.reshape(heads)

    scores = (
        jnp.einsum("qhd,khd->hqk", query_heads, key_heads, preferred_element_type=F32)
        * score_scale
    )
    softmax_out = jax.nn.softmax(scores, -1)
    softmax_low = softmax_out.astype(BF16)
    head_out = (
        jnp.einsum("hqk,khd->qhd", softmax_low, value_heads, preferred_element_type=F32)
        .astype(BF16)
        .reshape(row_count, group_width)
    )
    heads_all = lax.all_gather(head_out, "zl", axis=1, tiled=True)

    projection = gather_projection(w_out, n)
    order = feature_of_row(w_out.shape[1])
    spread = (order[:, None] == jnp.arange(features)[None, :]).astype(BF16)

    cot_pair = jnp.concatenate(by_core(cotangent, shift(cotangent, "core", 1)), 0)
    cot_pair = lax.dot_general(
        cot_pair, spread, (((1,), (1,)), ((), ())), preferred_element_type=F32
    ).astype(BF16)

    def part(group):
        columns = lax.dynamic_index_in_dim(projection, group % n, 0, keepdims=False)
        return jnp.dot(cot_pair, columns, preferred_element_type=F32).reshape(
            2, row_count, group_width
        )

    sign = 1 - 2 * core
    sums = None
    for step in range(1, n):
        term = part(me + sign * (n - step) + n)
        pairs = [(i, i + 1) for i in range(step)] + [
            (2 * n - 1 - i, 2 * n - 2 - i) for i in range(step)
        ]
        new = []
        for image in range(2):
            total = term[image] if sums is None else sums[image].astype(F32) + term[image]
            new.append(lax.ppermute(total.astype(BF16), CZ, pairs))
        sums = new
    first_sum, second_sum = sums
    own_sum = jnp.where(core == 0, first_sum, second_sum)
    their_sum = jnp.where(core == 0, second_sum, first_sum)
    other_sum = shift(their_sum, "core", 1)
    own_columns = lax.dynamic_index_in_dim(projection, me, 0, keepdims=False)
    own_cot = lax.dynamic_slice_in_dim(cot_pair, core * row_count, row_count, 0)
    own_part = jnp.dot(own_cot, own_columns, preferred_element_type=F32)
    grad_out = (own_part + own_sum.astype(F32) + other_sum.astype(F32)).astype(BF16)

    out_rows = lax.dot_general(
        heads_all.reshape(row_count, n, group_width),
        projection,
        (((1, 2), (0, 2)), ((), ())),
        preferred_element_type=F32,
    ).astype(BF16)
    branch_out = jnp.dot(out_rows, spread, preferred_element_type=F32).astype(BF16)

    grad_heads = grad_out.reshape(heads)
    soft_grad = jnp.einsum("qhd,khd->hqk", grad_heads, value_heads, preferred_element_type=F32)
    score_grad = (
        softmax_out * (soft_grad - jnp.sum(soft_grad * softmax_out, -1, keepdims=True))
    ).astype(BF16)

    def flat(value):
        return value.astype(BF16).reshape(row_count, group_width)

    grad_queries = flat(
        jnp.einsum("hqk,khd->qhd", score_grad, key_heads, preferred_element_type=F32) * score_scale
    )
    grad_keys = flat(
        jnp.einsum("hqk,qhd->khd", score_grad, query_heads, preferred_element_type=F32)
        * score_scale
    )
    grad_values = flat(
        jnp.einsum("hqk,qhd->khd", softmax_low, grad_heads, preferred_element_type=F32)
    )
    return (branch_out, grad_queries, grad_keys, grad_values)


def solution(mesh):
    fine = Mesh(mesh.devices.reshape(SIZES), (*DP, "zl"))
    tokens = P(DP, "zl")
    return jax.shard_map(
        on_device,
        mesh=fine,
        in_specs=(tokens, tokens, tokens, P(None, ("zl", *DP)), tokens),
        out_specs=(tokens, tokens, tokens, tokens),
        check_vma=False,
    )
```

```python
import math

import jax
import jax.numpy as jnp
import numpy as np
from jax import lax
from jax.sharding import Mesh, PartitionSpec as P

HD = 128
SEQ = 256
SIZES = (2, 8, 4, 2, 8)
DP = ("zh", "y", "x", "core")
BF16 = jnp.bfloat16
F32 = jnp.float32


def folded(n):
    return [*range(0, n, 2), *reversed(range(1, n, 2))]


def swap_core(block):
    return lax.ppermute(block, "core", [(0, 1), (1, 0)])


def by_core(own, other):
    first = lax.axis_index("core") == 0
    return jnp.where(first, own, other), jnp.where(first, other, own)


def feature_of_row(rows_dev):
    nz, ny, nx, nc = (lax.axis_size(a) for a in DP)
    y, z, x, c, r = np.indices((ny, nz, nx, nc, rows_dev)).reshape(5, -1)
    return (((z * ny + y) * nx + x) * nc + c) * rows_dev + r


def gather_projection(w_out):
    near = lax.all_gather(w_out.T, ("zh", "x", "core"), axis=0, tiled=True)
    half = near.shape[1] // 2
    mine = lax.dynamic_slice_in_dim(near, lax.axis_index("core") * half, half, 1)
    whole = lax.all_gather(mine, "y", axis=0, tiled=True)
    return jnp.concatenate(by_core(whole, swap_core(whole)), 1)


def on_device(queries, keys, values, w_out, cotangent):
    row_count = queries.shape[0]
    group_width = queries.shape[1]
    local_heads = group_width // HD
    n = lax.axis_size("zl")
    features = cotangent.shape[1]
    score_scale = 1.0 / math.sqrt(HD)
    heads = (row_count, local_heads, HD)
    query_heads = queries.reshape(heads)
    key_heads = keys.reshape(heads)
    value_heads = values.reshape(heads)

    scores = (
        jnp.einsum("qhd,khd->hqk", query_heads, key_heads, preferred_element_type=F32)
        * score_scale
    )
    softmax_out = jax.nn.softmax(scores, -1)
    softmax_low = softmax_out.astype(BF16)
    head_out = (
        jnp.einsum("hqk,khd->qhd", softmax_low, value_heads, preferred_element_type=F32)
        .astype(BF16)
        .reshape(row_count, group_width)
    )
    line = folded(n)
    heads_all = lax.all_gather(head_out, "zl", axis=1, tiled=True, axis_index_groups=[line])

    projection = gather_projection(w_out)
    order = jnp.asarray(feature_of_row(w_out.shape[1]))
    spread = (order[:, None] == jnp.arange(features)[None, :]).astype(BF16)
    cot_rows = lax.dot_general(
        cotangent, spread, (((1,), (1,)), ((), ())), preferred_element_type=F32
    ).astype(BF16)

    terms = jnp.dot(cot_rows, projection, preferred_element_type=F32).astype(BF16)
    terms = jnp.stack([terms[:, g * group_width : (g + 1) * group_width] for g in line], 0)
    grad_out = lax.psum_scatter(
        terms, "zl", scatter_dimension=0, tiled=False, axis_index_groups=[line]
    )

    heads_all = jnp.concatenate(
        [
            heads_all[:, line.index(g) * group_width : (line.index(g) + 1) * group_width]
            for g in range(n)
        ],
        1,
    )
    out_rows = lax.dot_general(
        heads_all, projection, (((1,), (1,)), ((), ())), preferred_element_type=F32
    ).astype(BF16)
    branch_out = jnp.dot(out_rows, spread, preferred_element_type=F32).astype(BF16)

    grad_heads = grad_out.reshape(heads)
    soft_grad = jnp.einsum("qhd,khd->hqk", grad_heads, value_heads, preferred_element_type=F32)
    score_grad = (
        softmax_out * (soft_grad - jnp.sum(soft_grad * softmax_out, -1, keepdims=True))
    ).astype(BF16)

    def flat(value):
        return value.astype(BF16).reshape(row_count, group_width)

    grad_queries = flat(
        jnp.einsum("hqk,khd->qhd", score_grad, key_heads, preferred_element_type=F32) * score_scale
    )
    grad_keys = flat(
        jnp.einsum("hqk,qhd->khd", score_grad, query_heads, preferred_element_type=F32)
        * score_scale
    )
    grad_values = flat(
        jnp.einsum("hqk,qhd->khd", softmax_low, grad_heads, preferred_element_type=F32)
    )
    return (branch_out, grad_queries, grad_keys, grad_values)


def solution(mesh):
    fine = Mesh(mesh.devices.reshape(SIZES), (*DP, "zl"))
    tokens = P(DP, "zl")
    return jax.shard_map(
        on_device,
        mesh=fine,
        in_specs=(tokens, tokens, tokens, P(None, ("zl", *DP)), tokens),
        out_specs=(tokens, tokens, tokens, tokens),
        check_vma=False,
    )
```

```python
import functools
import math

import jax
import jax.numpy as jnp
import numpy as np
from jax import lax
from jax.experimental import pallas as pl
from jax.experimental.pallas import tpu as pltpu
from jax.sharding import Mesh, PartitionSpec as P

HD = 128
SEQ = 256
SIZES = (2, 8, 4, 2, 8)
DP = ("zh", "y", "x", "core")
BF16 = jnp.bfloat16
F32 = jnp.float32
PARAMS = pltpu.CompilerParams(vmem_limit_bytes=40 * 1024 * 1024)
NT = (((1,), (1,)), ((), ()))
TN = (((0,), (0,)), ((), ()))


def folded(n):
    return [*range(0, n, 2), *reversed(range(1, n, 2))]


def shift(block, axis, by):
    n = lax.axis_size(axis)
    return lax.ppermute(block, axis, [(i, (i + by) % n) for i in range(n)])


def by_core(own, other):
    first = lax.axis_index("core") == 0
    return jnp.where(first, own, other), jnp.where(first, other, own)


def dot(a, b):
    return jnp.dot(a, b, preferred_element_type=F32)


def dot_nt(a, b):
    return lax.dot_general(a, b, NT, preferred_element_type=F32)


def dot_tn(a, b):
    return lax.dot_general(a, b, TN, preferred_element_type=F32)


def cost(flops, nbytes, transcendentals=0):
    return pl.CostEstimate(flops=flops, bytes_accessed=nbytes, transcendentals=transcendentals)


def forward_kernel(scale, q_ref, k_ref, v_ref, o_ref, p_ref):
    for head in range(q_ref.shape[1] // HD):
        cols = slice(head * HD, (head + 1) * HD)
        scores = dot_nt(q_ref[:, cols], k_ref[:, cols]) * scale
        powers = jnp.exp(scores - jnp.max(scores, axis=1, keepdims=True))
        soft = powers / jnp.sum(powers, axis=1, keepdims=True)
        p_ref[head] = soft
        o_ref[:, cols] = dot(soft.astype(BF16), v_ref[:, cols]).astype(BF16)


def backward_kernel(scale, q_ref, k_ref, v_ref, p_ref, g_ref, dq_ref, dk_ref, dv_ref):
    for head in range(q_ref.shape[1] // HD):
        cols = slice(head * HD, (head + 1) * HD)
        soft = p_ref[head]
        grad = g_ref[:, cols]
        soft_grad = dot_nt(grad, v_ref[:, cols])
        inner = jnp.sum(soft_grad * soft, axis=1, keepdims=True)
        score_grad = (soft * (soft_grad - inner)).astype(BF16)
        dv_ref[:, cols] = dot_tn(soft.astype(BF16), grad).astype(BF16)
        dq_ref[:, cols] = (dot(score_grad, k_ref[:, cols]) * scale).astype(BF16)
        dk_ref[:, cols] = (dot_tn(score_grad, q_ref[:, cols]) * scale).astype(BF16)


def terms_kernel(slot_ref, cot_ref, w_ref, *refs):
    refs[-1][0] = dot(cot_ref[...], w_ref[...]).astype(BF16)


def output_kernel(slots, core_ref, o_ref, own_ref, other_ref, sown_ref, sother_ref, out_ref):
    width = o_ref.shape[2]
    for core in range(2):

        @pl.when(core_ref[0] == core)
        def _():
            total = None
            for half, w_ref, s_ref in (
                (core, own_ref, sown_ref),
                (1 - core, other_ref, sother_ref),
            ):
                rows = sum(
                    dot_nt(o_ref[slot], w_ref[:, j * width : (j + 1) * width])
                    for j, slot in enumerate(slots[half])
                )
                placed = dot(rows.astype(BF16), s_ref[...])
                total = placed if total is None else total + placed
            out_ref[...] = total.astype(BF16)


def spread_of(rows_dev, features, core):
    nz, ny, nx, nc = (lax.axis_size(a) for a in DP)
    x0, z0 = lax.axis_index("x"), lax.axis_index("zh")
    place, x, z, c, r = np.indices((ny, nx, nz, nc, rows_dev)).reshape(5, -1)
    y = jnp.where(core == 0, place, ny - 1 - place)
    x = (x0 + x) % nx
    z = (z0 + z) % nz
    feature = (((z * ny + y) * nx + x) * nc + c) * rows_dev + r
    return (feature[:, None] == jnp.arange(features)[None, :]).astype(BF16)


def first_stage(w_out):
    shard = w_out.T
    core = lax.axis_index("core")
    half = shard.shape[1] // 2
    both = jnp.concatenate([shard, shift(shard, "zh", 1)], 0).reshape(2, *shard.shape)
    mine = lax.dynamic_slice_in_dim(both, core * half, half, 2)
    theirs = shift(lax.dynamic_slice_in_dim(both, (1 - core) * half, half, 2), "core", 1)
    base = jnp.stack(by_core(mine, theirs), 1).reshape(-1, half)
    nx = lax.axis_size("x")
    return jnp.concatenate([base] + [shift(base, "x", -i) for i in range(1, nx)], 0)


def on_device(queries, keys, values, w_out, cotangent):
    row_count, group_width = queries.shape
    features = cotangent.shape[1]
    local_heads = group_width // HD
    n = lax.axis_size("zl")
    ny = lax.axis_size("y")
    core = lax.axis_index("core")
    scale = 1.0 / math.sqrt(HD)
    line = folded(n)
    slots = [[line.index(h * n // 2 + j) for j in range(n // 2)] for h in range(2)]
    tokens = jax.ShapeDtypeStruct((row_count, group_width), BF16)

    attention_flops = 2 * row_count * row_count * group_width
    head_out, soft = pl.pallas_call(
        functools.partial(forward_kernel, scale),
        out_shape=(
            tokens,
            jax.ShapeDtypeStruct((local_heads, row_count, row_count), F32),
        ),
        compiler_params=PARAMS,
        cost_estimate=cost(2 * attention_flops, 1 << 21, local_heads * row_count**2),
        name="attention_forward",
    )(queries, keys, values)
    heads_all = lax.all_gather(head_out, "zl", axis=0, axis_index_groups=[line])

    w_out, head_out = lax.optimization_barrier((w_out, head_out))
    block = first_stage(w_out)
    ring = list(range(ny))
    own = lax.all_gather(
        block,
        ("core", "y"),
        axis=0,
        tiled=True,
        axis_index_groups=[ring, [2 * ny - 1 - i for i in ring]],
    )
    own, heads_all = lax.optimization_barrier((own, heads_all))
    other = shift(own, "core", 1)
    spread_own = spread_of(w_out.shape[1], features, core)
    spread_other = spread_of(w_out.shape[1], features, 1 - core)
    cot_own = dot_nt(cotangent, spread_own).astype(BF16)
    cot_other = dot_nt(cotangent, spread_other).astype(BF16)

    def terms(half, cot, columns, *into):
        places = jnp.where(half == 0, jnp.asarray(slots[0]), jnp.asarray(slots[1]))
        return pl.pallas_call(
            terms_kernel,
            out_shape=jax.ShapeDtypeStruct((n, row_count, group_width), BF16),
            grid_spec=pltpu.PrefetchScalarGridSpec(
                num_scalar_prefetch=1,
                grid=(n // 2,),
                in_specs=[
                    pl.BlockSpec((row_count, features), lambda j, place: (0, 0)),
                    pl.BlockSpec((features, group_width), lambda j, place: (0, j)),
                ]
                + [pl.BlockSpec(memory_space=pl.ANY)] * len(into),
                out_specs=pl.BlockSpec(
                    (1, row_count, group_width), lambda j, place: (place[j], 0, 0)
                ),
            ),
            input_output_aliases={3: 0} if into else {},
            compiler_params=PARAMS,
            cost_estimate=cost(row_count * features * group_width * n, 4 << 20),
            name="gradient_terms",
        )(places.astype(jnp.int32), cot, columns, *into)

    terms_all = terms(core, cot_own, own)
    terms_all = terms(1 - core, cot_other, other, terms_all)
    grad_out = lax.psum_scatter(
        terms_all, "zl", scatter_dimension=0, tiled=False, axis_index_groups=[line]
    )

    vmem = pl.BlockSpec(memory_space=pltpu.VMEM)
    branch_out = pl.pallas_call(
        functools.partial(output_kernel, slots),
        out_shape=jax.ShapeDtypeStruct((row_count, features), BF16),
        in_specs=[pl.BlockSpec(memory_space=pltpu.SMEM)] + [vmem] * 5,
        out_specs=vmem,
        compiler_params=PARAMS,
        cost_estimate=cost(2 * row_count * features * group_width * n, 8 << 20),
        name="output_projection",
    )(
        jnp.reshape(core, (1,)).astype(jnp.int32),
        heads_all,
        own,
        other,
        spread_own,
        spread_other,
    )

    grads = pl.pallas_call(
        functools.partial(backward_kernel, scale),
        out_shape=(tokens, tokens, tokens),
        compiler_params=PARAMS,
        cost_estimate=cost(4 * attention_flops, 1 << 21),
        name="attention_backward",
    )(queries, keys, values, soft, grad_out)
    return (branch_out, *grads)


def solution(mesh):
    fine = Mesh(mesh.devices.reshape(SIZES), (*DP, "zl"))
    tokens = P(DP, "zl")
    return jax.shard_map(
        on_device,
        mesh=fine,
        in_specs=(tokens, tokens, tokens, P(None, ("zl", *DP)), tokens),
        out_specs=(tokens, tokens, tokens, tokens),
        check_vma=False,
    )
```

```python
import functools
import math

import jax
import jax.numpy as jnp
import numpy as np
from jax import lax
from jax.experimental import pallas as pl
from jax.experimental.pallas import tpu as pltpu
from jax.sharding import Mesh, PartitionSpec as P

HD = 128
SEQ = 256
SIZES = (2, 8, 4, 2, 8)
DP = ("zh", "y", "x", "core")
BF16 = jnp.bfloat16
F32 = jnp.float32
PARAMS = pltpu.CompilerParams(vmem_limit_bytes=40 * 1024 * 1024)
WIDE = pltpu.CompilerParams(vmem_limit_bytes=60 * 1024 * 1024)
NT = (((1,), (1,)), ((), ()))
TN = (((0,), (0,)), ((), ()))


def folded(n):
    return [*range(0, n, 2), *reversed(range(1, n, 2))]


def shift(block, axis, by):
    n = lax.axis_size(axis)
    return lax.ppermute(block, axis, [(i, (i + by) % n) for i in range(n)])


def by_core(own, other):
    first = lax.axis_index("core") == 0
    return jnp.where(first, own, other), jnp.where(first, other, own)


def dot(a, b):
    return jnp.dot(a, b, preferred_element_type=F32)


def dot_nt(a, b):
    return lax.dot_general(a, b, NT, preferred_element_type=F32)


def dot_tn(a, b):
    return lax.dot_general(a, b, TN, preferred_element_type=F32)


def cost(flops, nbytes, transcendentals=0):
    return pl.CostEstimate(flops=flops, bytes_accessed=nbytes, transcendentals=transcendentals)


def forward_kernel(scale, q_ref, k_ref, v_ref, o_ref, p_ref):
    scores = dot_nt(q_ref[...], k_ref[...]) * scale
    powers = jnp.exp(scores - jnp.max(scores, axis=1, keepdims=True))
    soft = powers / jnp.sum(powers, axis=1, keepdims=True)
    p_ref[0] = soft
    o_ref[...] = dot(soft.astype(BF16), v_ref[...]).astype(BF16)


def backward_kernel(scale, q_ref, k_ref, v_ref, p_ref, g_ref, dq_ref, dk_ref, dv_ref):
    soft = p_ref[0]
    grad = g_ref[...]
    soft_grad = dot_nt(grad, v_ref[...])
    inner = jnp.sum(soft_grad * soft, axis=1, keepdims=True)
    score_grad = (soft * (soft_grad - inner)).astype(BF16)
    dv_ref[...] = dot_tn(soft.astype(BF16), grad).astype(BF16)
    dq_ref[...] = (dot(score_grad, k_ref[...]) * scale).astype(BF16)
    dk_ref[...] = (dot_tn(score_grad, q_ref[...]) * scale).astype(BF16)


def terms_kernel(slot_ref, cot_ref, near_ref, far_ref, *refs):
    near = near_ref.shape[0]
    total = dot(cot_ref[:, :near], near_ref[...]) + dot(cot_ref[:, near:], far_ref[...])
    refs[-1][0] = total.astype(BF16)


def output_kernel(slots, core_ref, o_ref, own_near, own_far, other_near, other_far, s_ref, out_ref):
    width = o_ref.shape[2]
    near = own_near.shape[0]
    for core in range(2):

        @pl.when(core_ref[0] == core)
        def _():
            total = None
            for place, (first, last) in ((0, (own_near, other_near)), (near, (own_far, other_far))):
                rows = None
                for half, w_ref in ((core, first), (1 - core, last)):
                    for j, slot in enumerate(slots[half]):
                        term = dot_nt(o_ref[slot], w_ref[:, j * width : (j + 1) * width])
                        rows = term if rows is None else rows + term
                placed = dot(rows.astype(BF16), s_ref[place : place + rows.shape[1], :])
                total = placed if total is None else total + placed
            out_ref[...] = total.astype(BF16)


def ring_offsets(n):
    offsets = [0]
    for step in range(1, n // 2 + 1):
        offsets.append(-step)
        if 2 * step < n:
            offsets.append(step)
    return np.array(offsets)


def ring_gather(block, axis, beside, join):
    n = lax.axis_size(axis)
    up = down = block
    blocks = [block]
    for step in range(1, n // 2 + 1):
        if step == join:
            up, beside = lax.optimization_barrier((up, beside))
        up = shift(up, axis, 1)
        blocks.append(up)
        if 2 * step < n:
            down = shift(down, axis, -1)
            blocks.append(down)
    return blocks, beside


def spread_of(rows_dev, features):
    nz, ny, nx, nc = (lax.axis_size(a) for a in DP)
    x0, y0, z0 = (lax.axis_index(a) for a in ("x", "y", "zh"))
    place, x, z, c, r = np.indices((ny, nx, nz, nc, rows_dev)).reshape(5, -1)
    y = (y0 + ny + ring_offsets(ny)[place]) % ny
    x = (x0 + x) % nx
    z = (z0 + z) % nz
    feature = (((z * ny + y) * nx + x) * nc + c) * rows_dev + r
    return (feature[:, None] == jnp.arange(features)[None, :]).astype(BF16)


def first_stage(shard, across):
    core = lax.axis_index("core")
    half = shard.shape[1] // 2
    both = jnp.concatenate([shard, across], 0).reshape(2, *shard.shape)
    mine = lax.dynamic_slice_in_dim(both, core * half, half, 2)
    theirs = shift(lax.dynamic_slice_in_dim(both, (1 - core) * half, half, 2), "core", 1)
    base = jnp.stack(by_core(mine, theirs), 1).reshape(-1, half)
    nx = lax.axis_size("x")
    return jnp.concatenate([base] + [shift(base, "x", -i) for i in range(1, nx)], 0)


def on_device(queries, keys, values, w_out, cotangent):
    row_count, group_width = queries.shape
    features = cotangent.shape[1]
    local_heads = group_width // HD
    n = lax.axis_size("zl")
    ny = lax.axis_size("y")
    core = lax.axis_index("core")
    scale = 1.0 / math.sqrt(HD)
    line = folded(n)
    slots = [[line.index(h * n // 2 + j) for j in range(n // 2)] for h in range(2)]
    tokens = jax.ShapeDtypeStruct((row_count, group_width), BF16)

    attention_flops = 2 * row_count * row_count * group_width
    head = pl.BlockSpec((row_count, HD), lambda h: (0, h))
    square = pl.BlockSpec((1, row_count, row_count), lambda h: (h, 0, 0))
    across = shift(w_out.T, "zh", 1)
    head_out, soft = pl.pallas_call(
        functools.partial(forward_kernel, scale),
        out_shape=(
            tokens,
            jax.ShapeDtypeStruct((local_heads, row_count, row_count), F32),
        ),
        grid=(local_heads,),
        in_specs=[head] * 3,
        out_specs=(head, square),
        compiler_params=WIDE,
        cost_estimate=cost(2 * attention_flops, 1 << 21, local_heads * row_count**2),
        name="attention_forward",
    )(queries, keys, values)
    heads_all = lax.all_gather(head_out, "zl", axis=0, axis_index_groups=[line])
    spread = spread_of(w_out.shape[1], features)
    cot_rows = dot_nt(cotangent, spread).astype(BF16)

    across, head_out, cot_rows = lax.optimization_barrier((across, head_out, cot_rows))
    blocks, heads_all = ring_gather(first_stage(w_out.T, across), "y", heads_all, 4)
    early = 2 * ((ny + 2) // 4) + 1
    own_near = jnp.concatenate(blocks[:early], 0)
    other_near = shift(own_near, "core", 1)
    own_far = jnp.concatenate(blocks[early:], 0)
    other_far = shift(own_far, "core", 1)

    def terms(half, near, far, *into):
        places = jnp.where(half == 0, jnp.asarray(slots[0]), jnp.asarray(slots[1]))
        return pl.pallas_call(
            terms_kernel,
            out_shape=jax.ShapeDtypeStruct((n, row_count, group_width), BF16),
            grid_spec=pltpu.PrefetchScalarGridSpec(
                num_scalar_prefetch=1,
                grid=(n // 2,),
                in_specs=[
                    pl.BlockSpec((row_count, features), lambda j, place: (0, 0)),
                    pl.BlockSpec((near.shape[0], group_width), lambda j, place: (0, j)),
                    pl.BlockSpec((far.shape[0], group_width), lambda j, place: (0, j)),
                ]
                + [pl.BlockSpec(memory_space=pl.ANY)] * len(into),
                out_specs=pl.BlockSpec(
                    (1, row_count, group_width), lambda j, place: (place[j], 0, 0)
                ),
            ),
            input_output_aliases={4: 0} if into else {},
            compiler_params=PARAMS,
            cost_estimate=cost(row_count * features * group_width * n, 4 << 20),
            name="gradient_terms",
        )(places.astype(jnp.int32), cot_rows, near, far, *into)

    terms_all = terms(core, own_near, own_far)
    terms_all = terms(1 - core, other_near, other_far, terms_all)
    grad_out = lax.psum_scatter(
        terms_all, "zl", scatter_dimension=0, tiled=False, axis_index_groups=[line]
    )

    vmem = pl.BlockSpec(memory_space=pltpu.VMEM)
    branch_out = pl.pallas_call(
        functools.partial(output_kernel, slots),
        out_shape=jax.ShapeDtypeStruct((row_count, features), BF16),
        in_specs=[pl.BlockSpec(memory_space=pltpu.SMEM)] + [vmem] * 6,
        out_specs=vmem,
        compiler_params=PARAMS,
        cost_estimate=cost(2 * row_count * features * group_width * n, 8 << 20),
        name="output_projection",
    )(
        jnp.reshape(core, (1,)).astype(jnp.int32),
        heads_all,
        own_near,
        own_far,
        other_near,
        other_far,
        spread,
    )

    grads = pl.pallas_call(
        functools.partial(backward_kernel, scale),
        out_shape=(tokens, tokens, tokens),
        grid=(local_heads,),
        in_specs=[head] * 3 + [square, head],
        out_specs=(head, head, head),
        compiler_params=WIDE,
        cost_estimate=cost(4 * attention_flops, 1 << 21),
        name="attention_backward",
    )(queries, keys, values, soft, grad_out)
    return (branch_out, *grads)


def solution(mesh):
    fine = Mesh(mesh.devices.reshape(SIZES), (*DP, "zl"))
    tokens = P(DP, "zl")
    return jax.shard_map(
        on_device,
        mesh=fine,
        in_specs=(tokens, tokens, tokens, P(None, ("zl", *DP)), tokens),
        out_specs=(tokens, tokens, tokens, tokens),
        check_vma=False,
    )
```

```python
import functools
import math

import jax
import jax.numpy as jnp
import numpy as np
from jax import lax
from jax.experimental import pallas as pl
from jax.experimental.pallas import tpu as pltpu
from jax.sharding import Mesh, PartitionSpec as P

HD = 128
SEQ = 256
SIZES = (2, 8, 4, 2, 8)
DP = ("zh", "y", "x", "core")
BF16 = jnp.bfloat16
F32 = jnp.float32
PARAMS = pltpu.CompilerParams(vmem_limit_bytes=40 * 1024 * 1024)
WIDE = pltpu.CompilerParams(vmem_limit_bytes=60 * 1024 * 1024)
NT = (((1,), (1,)), ((), ()))
TN = (((0,), (0,)), ((), ()))


def folded(n):
    return [*range(0, n, 2), *reversed(range(1, n, 2))]


def shift(block, axis, by):
    n = lax.axis_size(axis)
    return lax.ppermute(block, axis, [(i, (i + by) % n) for i in range(n)])


def by_core(own, other):
    first = lax.axis_index("core") == 0
    return jnp.where(first, own, other), jnp.where(first, other, own)


def dot(a, b):
    return jnp.dot(a, b, preferred_element_type=F32)


def dot_nt(a, b):
    return lax.dot_general(a, b, NT, preferred_element_type=F32)


def dot_tn(a, b):
    return lax.dot_general(a, b, TN, preferred_element_type=F32)


def cost(flops, nbytes, transcendentals=0):
    return pl.CostEstimate(flops=flops, bytes_accessed=nbytes, transcendentals=transcendentals)


def forward_kernel(scale, q_ref, k_ref, v_ref, o_ref, p_ref):
    scores = dot_nt(q_ref[...], k_ref[...]) * scale
    powers = jnp.exp(scores - jnp.max(scores, axis=1, keepdims=True))
    soft = powers / jnp.sum(powers, axis=1, keepdims=True)
    p_ref[0] = soft
    o_ref[...] = dot(soft.astype(BF16), v_ref[...]).astype(BF16)


def backward_kernel(scale, q_ref, k_ref, v_ref, p_ref, g_ref, dq_ref, dk_ref, dv_ref):
    soft = p_ref[0]
    grad = g_ref[...]
    soft_grad = dot_nt(grad, v_ref[...])
    inner = jnp.sum(soft_grad * soft, axis=1, keepdims=True)
    score_grad = (soft * (soft_grad - inner)).astype(BF16)
    dv_ref[...] = dot_tn(soft.astype(BF16), grad).astype(BF16)
    dq_ref[...] = (dot(score_grad, k_ref[...]) * scale).astype(BF16)
    dk_ref[...] = (dot_tn(score_grad, q_ref[...]) * scale).astype(BF16)


def sums_kernel(cot_ref, near_ref, out_ref):
    out_ref[...] = dot(cot_ref[:, : near_ref.shape[0]], near_ref[...])


def terms_kernel(
    slots, at_ref, cot_ref, own_sum, other_sum, own_mid, own_last, other_mid, other_last, out_ref
):
    width = out_ref.shape[2]
    last = cot_ref.shape[1] - own_last.shape[0]
    mid = last - own_mid.shape[0]
    for core in range(2):

        @pl.when(at_ref[0] == core)
        def _():
            for half, sum_ref, mid_ref, last_ref in (
                (core, own_sum, own_mid, own_last),
                (1 - core, other_sum, other_mid, other_last),
            ):
                for i, slot in enumerate(slots[half]):
                    cols = pl.ds(pl.multiple_of((2 * i + at_ref[1]) * width, width), width)
                    term = sum_ref[:, cols] + dot(cot_ref[:, mid:last], mid_ref[:, cols])
                    term += dot(cot_ref[:, last:], last_ref[:, cols])
                    out_ref[slot] = term.astype(BF16)


def output_kernel(
    slots, core_ref, o_ref, own_near, own_mid, own_last, other_near, other_mid, other_last, s_ref, out_ref
):
    width = o_ref.shape[2]
    for core in range(2):

        @pl.when(core_ref[0] == core)
        def _():
            total, place = None, 0
            for first, last in (
                (own_near, other_near),
                (own_mid, other_mid),
                (own_last, other_last),
            ):
                rows = None
                for half, w_ref in ((core, first), (1 - core, last)):
                    for j, slot in enumerate(slots[half]):
                        term = dot_nt(o_ref[slot], w_ref[:, j * width : (j + 1) * width])
                        rows = term if rows is None else rows + term
                placed = dot(rows.astype(BF16), s_ref[place : place + rows.shape[1], :])
                total = placed if total is None else total + placed
                place += rows.shape[1]
            out_ref[...] = total.astype(BF16)


def ring_offsets(n):
    offsets = [0]
    for step in range(1, n // 2 + 1):
        offsets.append(-step)
        if 2 * step < n:
            offsets.append(step)
    return np.array(offsets)


def ring_gather(block, axis):
    n = lax.axis_size(axis)
    up = down = block
    blocks = [block]
    for step in range(1, n // 2 + 1):
        up = shift(up, axis, 1)
        blocks.append(up)
        if 2 * step < n:
            down = shift(down, axis, -1)
            blocks.append(down)
    return blocks


def spread_of(rows_dev, features):
    nz, ny, nx, nc = (lax.axis_size(a) for a in DP)
    x0, y0, z0 = (lax.axis_index(a) for a in ("x", "y", "zh"))
    place, x, z, c, r = np.indices((ny, nx, nz, nc, rows_dev)).reshape(5, -1)
    y = (y0 + ny + ring_offsets(ny)[place]) % ny
    x = (x0 + x) % nx
    z = (z0 + z) % nz
    feature = (((z * ny + y) * nx + x) * nc + c) * rows_dev + r
    return (feature[:, None] == jnp.arange(features)[None, :]).astype(BF16)


def first_stage(shard, across):
    core = lax.axis_index("core")
    half = shard.shape[1] // 2
    both = jnp.concatenate([shard, across], 0).reshape(2, *shard.shape)
    mine = lax.dynamic_slice_in_dim(both, core * half, half, 2)
    theirs = shift(lax.dynamic_slice_in_dim(both, (1 - core) * half, half, 2), "core", 1)
    base = jnp.stack(by_core(mine, theirs), 1).reshape(-1, half)
    nx = lax.axis_size("x")
    return jnp.concatenate([base] + [shift(base, "x", -i) for i in range(1, nx)], 0)


def on_device(queries, keys, values, w_out, cotangent):
    row_count, group_width = queries.shape
    features = cotangent.shape[1]
    local_heads = group_width // HD
    n = lax.axis_size("zl")
    ny = lax.axis_size("y")
    core = lax.axis_index("core")
    scale = 1.0 / math.sqrt(HD)
    half_line = folded(n // 2)
    same_parity = [[2 * m + q for m in half_line] for q in range(2)]
    pairs = [(i, i ^ 1) for i in range(n)]
    parity = lax.axis_index("zl") % 2
    slots = [
        [2 * half_line.index((h * n // 2 + j) // 2) + j % 2 for j in range(n // 2)]
        for h in range(2)
    ]
    tokens = jax.ShapeDtypeStruct((row_count, group_width), BF16)

    attention_flops = 2 * row_count * row_count * group_width
    head = pl.BlockSpec((row_count, HD), lambda h: (0, h))
    square = pl.BlockSpec((1, row_count, row_count), lambda h: (h, 0, 0))
    across = shift(w_out.T, "zh", 1)
    head_out, soft = pl.pallas_call(
        functools.partial(forward_kernel, scale),
        out_shape=(
            tokens,
            jax.ShapeDtypeStruct((local_heads, row_count, row_count), F32),
        ),
        grid=(local_heads,),
        in_specs=[head] * 3,
        out_specs=(head, square),
        compiler_params=WIDE,
        cost_estimate=cost(2 * attention_flops, 1 << 21, local_heads * row_count**2),
        name="attention_forward",
    )(queries, keys, values)
    pair_out = lax.ppermute(head_out, "zl", pairs)
    heads_pair = jnp.stack(
        [
            jnp.where(parity == 0, head_out, pair_out),
            jnp.where(parity == 0, pair_out, head_out),
        ],
        0,
    )
    heads_all = lax.all_gather(
        heads_pair, "zl", axis=0, tiled=True, axis_index_groups=same_parity
    )
    spread = spread_of(w_out.shape[1], features)
    cot_rows = dot_nt(cotangent, spread).astype(BF16)

    across, head_out, cot_rows = lax.optimization_barrier((across, head_out, cot_rows))
    blocks = ring_gather(first_stage(w_out.T, across), "y")
    early = 2 * ((ny + 2) // 4) + 1
    vmem = pl.BlockSpec(memory_space=pltpu.VMEM)
    smem = pl.BlockSpec(memory_space=pltpu.SMEM)

    def sums(near):
        return pl.pallas_call(
            sums_kernel,
            out_shape=jax.ShapeDtypeStruct((row_count, near.shape[1]), F32),
            in_specs=[vmem] * 2,
            out_specs=vmem,
            compiler_params=PARAMS,
            cost_estimate=cost(row_count * features * group_width * n, 4 << 20),
            name="gradient_sums",
        )(cot_rows, near)

    own_near = jnp.concatenate(blocks[:early], 0)
    other_near = shift(own_near, "core", 1)
    own_mid = jnp.concatenate(blocks[early:-1], 0)
    other_mid = shift(own_mid, "core", 1)
    own_sum = sums(own_near)
    other_sum = sums(other_near)
    own_last, own_sum, other_sum = lax.optimization_barrier(
        (blocks[-1], own_sum, other_sum)
    )
    other_last = shift(own_last, "core", 1)

    pair_slots = [[half_line.index(h * n // 4 + i) for i in range(n // 4)] for h in range(2)]

    def terms(which):
        return pl.pallas_call(
            functools.partial(terms_kernel, pair_slots),
            out_shape=jax.ShapeDtypeStruct((n // 2, row_count, group_width), BF16),
            in_specs=[smem] + [vmem] * 7,
            out_specs=vmem,
            compiler_params=PARAMS,
            cost_estimate=cost(row_count * own_last.shape[0] * group_width * n, 4 << 20),
            name="gradient_terms",
        )(
            jnp.stack([core, which]).astype(jnp.int32),
            cot_rows,
            own_sum,
            other_sum,
            own_mid,
            own_last,
            other_mid,
            other_last,
        )

    came = lax.ppermute(terms(1 - parity), "zl", pairs)
    came, heads_all = lax.optimization_barrier((came, heads_all))
    pair_terms = (terms(parity).astype(F32) + came.astype(F32)).astype(BF16)
    grad_out = lax.psum_scatter(
        pair_terms,
        "zl",
        scatter_dimension=0,
        tiled=False,
        axis_index_groups=same_parity,
    )

    branch_out = pl.pallas_call(
        functools.partial(output_kernel, slots),
        out_shape=jax.ShapeDtypeStruct((row_count, features), BF16),
        in_specs=[smem] + [vmem] * 8,
        out_specs=vmem,
        compiler_params=PARAMS,
        cost_estimate=cost(2 * row_count * features * group_width * n, 8 << 20),
        name="output_projection",
    )(
        jnp.reshape(core, (1,)).astype(jnp.int32),
        heads_all,
        own_near,
        own_mid,
        own_last,
        other_near,
        other_mid,
        other_last,
        spread,
    )

    grads = pl.pallas_call(
        functools.partial(backward_kernel, scale),
        out_shape=(tokens, tokens, tokens),
        grid=(local_heads,),
        in_specs=[head] * 3 + [square, head],
        out_specs=(head, head, head),
        compiler_params=WIDE,
        cost_estimate=cost(4 * attention_flops, 1 << 21),
        name="attention_backward",
    )(queries, keys, values, soft, grad_out)
    return (branch_out, *grads)


def solution(mesh):
    fine = Mesh(mesh.devices.reshape(SIZES), (*DP, "zl"))
    tokens = P(DP, "zl")
    return jax.shard_map(
        on_device,
        mesh=fine,
        in_specs=(tokens, tokens, tokens, P(None, ("zl", *DP)), tokens),
        out_specs=(tokens, tokens, tokens, tokens),
        check_vma=False,
    )
```

```python
import functools
import math

import jax
import jax.numpy as jnp
import numpy as np
from jax import lax
from jax.experimental import pallas as pl
from jax.experimental.pallas import tpu as pltpu
from jax.sharding import Mesh, PartitionSpec as P

HD = 128
SEQ = 256
SIZES = (2, 8, 4, 2, 8)
DP = ("zh", "y", "x", "core")
BF16 = jnp.bfloat16
F32 = jnp.float32
PARAMS = pltpu.CompilerParams(vmem_limit_bytes=40 * 1024 * 1024)
WIDE = pltpu.CompilerParams(vmem_limit_bytes=60 * 1024 * 1024)
NT = (((1,), (1,)), ((), ()))
TN = (((0,), (0,)), ((), ()))


def folded(n):
    return [*range(0, n, 2), *reversed(range(1, n, 2))]


def shift(block, axis, by):
    n = lax.axis_size(axis)
    return lax.ppermute(block, axis, [(i, (i + by) % n) for i in range(n)])


def by_core(own, other):
    first = lax.axis_index("core") == 0
    return jnp.where(first, own, other), jnp.where(first, other, own)


def dot(a, b):
    return jnp.dot(a, b, preferred_element_type=F32)


def dot_nt(a, b):
    return lax.dot_general(a, b, NT, preferred_element_type=F32)


def dot_tn(a, b):
    return lax.dot_general(a, b, TN, preferred_element_type=F32)


def cost(flops, nbytes, transcendentals=0):
    return pl.CostEstimate(flops=flops, bytes_accessed=nbytes, transcendentals=transcendentals)


def forward_kernel(scale, q_ref, k_ref, v_ref, o_ref, p_ref):
    scores = dot_nt(q_ref[...], k_ref[...]) * scale
    powers = jnp.exp(scores - jnp.max(scores, axis=1, keepdims=True))
    soft = powers / jnp.sum(powers, axis=1, keepdims=True)
    p_ref[0] = soft
    o_ref[...] = dot(soft.astype(BF16), v_ref[...]).astype(BF16)


def backward_kernel(scale, q_ref, k_ref, v_ref, p_ref, g_ref, dq_ref, dk_ref, dv_ref):
    soft = p_ref[0]
    grad = g_ref[...]
    soft_grad = dot_nt(grad, v_ref[...])
    inner = jnp.sum(soft_grad * soft, axis=1, keepdims=True)
    score_grad = (soft * (soft_grad - inner)).astype(BF16)
    dv_ref[...] = dot_tn(soft.astype(BF16), grad).astype(BF16)
    dq_ref[...] = (dot(score_grad, k_ref[...]) * scale).astype(BF16)
    dk_ref[...] = (dot_tn(score_grad, q_ref[...]) * scale).astype(BF16)


def sums_kernel(cot_ref, near_ref, out_ref):
    out_ref[...] = dot(cot_ref[:, : near_ref.shape[0]], near_ref[...])


def terms_kernel(
    slots, core_ref, cot_ref, own_sum, other_sum, own_far, other_far, out_ref
):
    width = out_ref.shape[2]
    near = cot_ref.shape[1] - own_far.shape[0]
    for core in range(2):

        @pl.when(core_ref[0] == core)
        def _():
            for half, sum_ref, far_ref in (
                (core, own_sum, own_far),
                (1 - core, other_sum, other_far),
            ):
                for j, slot in enumerate(slots[half]):
                    cols = slice(j * width, (j + 1) * width)
                    term = sum_ref[:, cols] + dot(cot_ref[:, near:], far_ref[:, cols])
                    out_ref[slot] = term.astype(BF16)


def output_kernel(slots, core_ref, o_ref, own_near, own_far, other_near, other_far, s_ref, out_ref):
    width = o_ref.shape[2]
    near = own_near.shape[0]
    for core in range(2):

        @pl.when(core_ref[0] == core)
        def _():
            total = None
            for place, (first, last) in ((0, (own_near, other_near)), (near, (own_far, other_far))):
                rows = None
                for half, w_ref in ((core, first), (1 - core, last)):
                    for j, slot in enumerate(slots[half]):
                        term = dot_nt(o_ref[slot], w_ref[:, j * width : (j + 1) * width])
                        rows = term if rows is None else rows + term
                placed = dot(rows.astype(BF16), s_ref[place : place + rows.shape[1], :])
                total = placed if total is None else total + placed
            out_ref[...] = total.astype(BF16)


def ring_offsets(n):
    offsets = [0]
    for step in range(1, n // 2 + 1):
        offsets.append(-step)
        if 2 * step < n:
            offsets.append(step)
    return np.array(offsets)


def ring_gather(block, axis, beside, join):
    n = lax.axis_size(axis)
    up = down = block
    blocks = [block]
    for step in range(1, n // 2 + 1):
        if step == join:
            up, beside = lax.optimization_barrier((up, beside))
        up = shift(up, axis, 1)
        blocks.append(up)
        if 2 * step < n:
            down = shift(down, axis, -1)
            blocks.append(down)
    return blocks, beside


def spread_of(rows_dev, features):
    nz, ny, nx, nc = (lax.axis_size(a) for a in DP)
    x0, y0, z0 = (lax.axis_index(a) for a in ("x", "y", "zh"))
    place, x, z, c, r = np.indices((ny, nx, nz, nc, rows_dev)).reshape(5, -1)
    y = (y0 + ny + ring_offsets(ny)[place]) % ny
    x = (x0 + x) % nx
    z = (z0 + z) % nz
    feature = (((z * ny + y) * nx + x) * nc + c) * rows_dev + r
    return (feature[:, None] == jnp.arange(features)[None, :]).astype(BF16)


def first_stage(shard, across):
    core = lax.axis_index("core")
    half = shard.shape[1] // 2
    both = jnp.concatenate([shard, across], 0).reshape(2, *shard.shape)
    mine = lax.dynamic_slice_in_dim(both, core * half, half, 2)
    theirs = shift(lax.dynamic_slice_in_dim(both, (1 - core) * half, half, 2), "core", 1)
    base = jnp.stack(by_core(mine, theirs), 1).reshape(-1, half)
    nx = lax.axis_size("x")
    return jnp.concatenate([base] + [shift(base, "x", -i) for i in range(1, nx)], 0)


def on_device(queries, keys, values, w_out, cotangent):
    row_count, group_width = queries.shape
    features = cotangent.shape[1]
    local_heads = group_width // HD
    n = lax.axis_size("zl")
    ny = lax.axis_size("y")
    core = lax.axis_index("core")
    scale = 1.0 / math.sqrt(HD)
    line = folded(n)
    slots = [[line.index(h * n // 2 + j) for j in range(n // 2)] for h in range(2)]
    tokens = jax.ShapeDtypeStruct((row_count, group_width), BF16)

    attention_flops = 2 * row_count * row_count * group_width
    head = pl.BlockSpec((row_count, HD), lambda h: (0, h))
    square = pl.BlockSpec((1, row_count, row_count), lambda h: (h, 0, 0))
    across = shift(w_out.T, "zh", 1)
    head_out, soft = pl.pallas_call(
        functools.partial(forward_kernel, scale),
        out_shape=(
            tokens,
            jax.ShapeDtypeStruct((local_heads, row_count, row_count), F32),
        ),
        grid=(local_heads,),
        in_specs=[head] * 3,
        out_specs=(head, square),
        compiler_params=WIDE,
        cost_estimate=cost(2 * attention_flops, 1 << 21, local_heads * row_count**2),
        name="attention_forward",
    )(queries, keys, values)
    heads_all = lax.all_gather(head_out, "zl", axis=0, axis_index_groups=[line])
    spread = spread_of(w_out.shape[1], features)
    cot_rows = dot_nt(cotangent, spread).astype(BF16)

    across, head_out, cot_rows = lax.optimization_barrier((across, head_out, cot_rows))
    blocks, heads_all = ring_gather(first_stage(w_out.T, across), "y", heads_all, 4)
    vmem = pl.BlockSpec(memory_space=pltpu.VMEM)
    smem = pl.BlockSpec(memory_space=pltpu.SMEM)

    def sums(near):
        return pl.pallas_call(
            sums_kernel,
            out_shape=jax.ShapeDtypeStruct((row_count, near.shape[1]), F32),
            in_specs=[vmem] * 2,
            out_specs=vmem,
            compiler_params=PARAMS,
            cost_estimate=cost(row_count * features * group_width * n, 4 << 20),
            name="gradient_sums",
        )(cot_rows, near)

    early = 2 * ((ny + 2) // 4) + 1
    own_near = jnp.concatenate(blocks[:early], 0)
    other_near = shift(own_near, "core", 1)
    own_sum = sums(own_near)
    other_sum = sums(other_near)
    own_far = jnp.concatenate(blocks[early:], 0)
    other_far = shift(own_far, "core", 1)

    terms_all = pl.pallas_call(
        functools.partial(terms_kernel, slots),
        out_shape=jax.ShapeDtypeStruct((n, row_count, group_width), BF16),
        in_specs=[smem] + [vmem] * 5,
        out_specs=vmem,
        compiler_params=PARAMS,
        cost_estimate=cost(2 * row_count * features * group_width * n, 8 << 20),
        name="gradient_terms",
    )(
        jnp.reshape(core, (1,)).astype(jnp.int32),
        cot_rows,
        own_sum,
        other_sum,
        own_far,
        other_far,
    )
    grad_out = lax.psum_scatter(
        terms_all, "zl", scatter_dimension=0, tiled=False, axis_index_groups=[line]
    )

    vmem = pl.BlockSpec(memory_space=pltpu.VMEM)
    branch_out = pl.pallas_call(
        functools.partial(output_kernel, slots),
        out_shape=jax.ShapeDtypeStruct((row_count, features), BF16),
        in_specs=[pl.BlockSpec(memory_space=pltpu.SMEM)] + [vmem] * 6,
        out_specs=vmem,
        compiler_params=PARAMS,
        cost_estimate=cost(2 * row_count * features * group_width * n, 8 << 20),
        name="output_projection",
    )(
        jnp.reshape(core, (1,)).astype(jnp.int32),
        heads_all,
        own_near,
        own_far,
        other_near,
        other_far,
        spread,
    )

    grads = pl.pallas_call(
        functools.partial(backward_kernel, scale),
        out_shape=(tokens, tokens, tokens),
        grid=(local_heads,),
        in_specs=[head] * 3 + [square, head],
        out_specs=(head, head, head),
        compiler_params=WIDE,
        cost_estimate=cost(4 * attention_flops, 1 << 21),
        name="attention_backward",
    )(queries, keys, values, soft, grad_out)
    return (branch_out, *grads)


def solution(mesh):
    fine = Mesh(mesh.devices.reshape(SIZES), (*DP, "zl"))
    tokens = P(DP, "zl")
    return jax.shard_map(
        on_device,
        mesh=fine,
        in_specs=(tokens, tokens, tokens, P(None, ("zl", *DP)), tokens),
        out_specs=(tokens, tokens, tokens, tokens),
        check_vma=False,
    )
```

```python
import functools
import math

import jax
import jax.numpy as jnp
import numpy as np
from jax import lax
from jax.experimental import pallas as pl
from jax.experimental.pallas import tpu as pltpu
from jax.sharding import Mesh, PartitionSpec as P

HD = 128
SEQ = 256
SIZES = (2, 8, 4, 2, 8)
DP = ("zh", "y", "x", "core")
BF16 = jnp.bfloat16
F32 = jnp.float32
PARAMS = pltpu.CompilerParams(vmem_limit_bytes=40 * 1024 * 1024)
WIDE = pltpu.CompilerParams(vmem_limit_bytes=60 * 1024 * 1024)
NT = (((1,), (1,)), ((), ()))
TN = (((0,), (0,)), ((), ()))


def folded(n):
    return [*range(0, n, 2), *reversed(range(1, n, 2))]


def shift(block, axis, by):
    n = lax.axis_size(axis)
    return lax.ppermute(block, axis, [(i, (i + by) % n) for i in range(n)])


def by_core(own, other):
    first = lax.axis_index("core") == 0
    return jnp.where(first, own, other), jnp.where(first, other, own)


def dot(a, b):
    return jnp.dot(a, b, preferred_element_type=F32)


def dot_nt(a, b):
    return lax.dot_general(a, b, NT, preferred_element_type=F32)


def dot_tn(a, b):
    return lax.dot_general(a, b, TN, preferred_element_type=F32)


def cost(flops, nbytes, transcendentals=0):
    return pl.CostEstimate(flops=flops, bytes_accessed=nbytes, transcendentals=transcendentals)


def forward_kernel(scale, q_ref, k_ref, v_ref, o_ref, p_ref):
    scores = dot_nt(q_ref[...], k_ref[...]) * scale
    powers = jnp.exp(scores - jnp.max(scores, axis=1, keepdims=True))
    soft = powers / jnp.sum(powers, axis=1, keepdims=True)
    p_ref[0] = soft
    o_ref[...] = dot(soft.astype(BF16), v_ref[...]).astype(BF16)


def backward_kernel(scale, q_ref, k_ref, v_ref, p_ref, g_ref, dq_ref, dk_ref, dv_ref):
    for head in range(q_ref.shape[1] // HD):
        cols = slice(head * HD, (head + 1) * HD)
        soft = p_ref[head]
        grad = g_ref[:, cols]
        soft_grad = dot_nt(grad, v_ref[:, cols])
        inner = jnp.sum(soft_grad * soft, axis=1, keepdims=True)
        score_grad = (soft * (soft_grad - inner)).astype(BF16)
        dv_ref[:, cols] = dot_tn(soft.astype(BF16), grad).astype(BF16)
        dq_ref[:, cols] = (dot(score_grad, k_ref[:, cols]) * scale).astype(BF16)
        dk_ref[:, cols] = (dot_tn(score_grad, q_ref[:, cols]) * scale).astype(BF16)


def sums_kernel(cot_ref, near_ref, out_ref):
    out_ref[...] = dot(cot_ref[:, : near_ref.shape[0]], near_ref[...])


def terms_kernel(
    slots, core_ref, cot_ref, own_sum, other_sum, own_far, other_far, out_ref
):
    width = out_ref.shape[2]
    near = cot_ref.shape[1] - own_far.shape[0]
    for core in range(2):

        @pl.when(core_ref[0] == core)
        def _():
            for half, sum_ref, far_ref in (
                (core, own_sum, own_far),
                (1 - core, other_sum, other_far),
            ):
                for j, slot in enumerate(slots[half]):
                    cols = slice(j * width, (j + 1) * width)
                    term = sum_ref[:, cols] + dot(cot_ref[:, near:], far_ref[:, cols])
                    out_ref[slot] = term.astype(BF16)


def output_kernel(slots, core_ref, o_ref, own_near, own_far, other_near, other_far, s_ref, out_ref):
    width = o_ref.shape[2]
    near = own_near.shape[0]
    for core in range(2):

        @pl.when(core_ref[0] == core)
        def _():
            total = None
            for place, (first, last) in ((0, (own_near, other_near)), (near, (own_far, other_far))):
                rows = None
                for half, w_ref in ((core, first), (1 - core, last)):
                    for j, slot in enumerate(slots[half]):
                        term = dot_nt(o_ref[slot], w_ref[:, j * width : (j + 1) * width])
                        rows = term if rows is None else rows + term
                placed = dot(rows.astype(BF16), s_ref[place : place + rows.shape[1], :])
                total = placed if total is None else total + placed
            out_ref[...] = total.astype(BF16)


def ring_offsets(n):
    offsets = [0]
    for step in range(1, n // 2 + 1):
        offsets.append(-step)
        if 2 * step < n:
            offsets.append(step)
    return np.array(offsets)


def ring_gather(block, axis, beside, join):
    n = lax.axis_size(axis)
    up = down = block
    blocks = [block]
    for step in range(1, n // 2 + 1):
        if step == join:
            up, beside = lax.optimization_barrier((up, beside))
        up = shift(up, axis, 1)
        blocks.append(up)
        if 2 * step < n:
            down = shift(down, axis, -1)
            blocks.append(down)
    return blocks, beside


def spread_of(rows_dev, features):
    nz, ny, nx, nc = (lax.axis_size(a) for a in DP)
    x0, y0, z0 = (lax.axis_index(a) for a in ("x", "y", "zh"))
    place, x, z, c, r = np.indices((ny, nx, nz, nc, rows_dev)).reshape(5, -1)
    y = (y0 + ny + ring_offsets(ny)[place]) % ny
    x = (x0 + x) % nx
    z = (z0 + z) % nz
    feature = (((z * ny + y) * nx + x) * nc + c) * rows_dev + r
    return (feature[:, None] == jnp.arange(features)[None, :]).astype(BF16)


def first_stage(shard, across):
    core = lax.axis_index("core")
    half = shard.shape[1] // 2
    both = jnp.concatenate([shard, across], 0).reshape(2, *shard.shape)
    mine = lax.dynamic_slice_in_dim(both, core * half, half, 2)
    theirs = shift(lax.dynamic_slice_in_dim(both, (1 - core) * half, half, 2), "core", 1)
    base = jnp.stack(by_core(mine, theirs), 1).reshape(-1, half)
    nx = lax.axis_size("x")
    return jnp.concatenate([base] + [shift(base, "x", -i) for i in range(1, nx)], 0)


def on_device(queries, keys, values, w_out, cotangent):
    row_count, group_width = queries.shape
    features = cotangent.shape[1]
    local_heads = group_width // HD
    n = lax.axis_size("zl")
    ny = lax.axis_size("y")
    core = lax.axis_index("core")
    scale = 1.0 / math.sqrt(HD)
    line = folded(n)
    slots = [[line.index(h * n // 2 + j) for j in range(n // 2)] for h in range(2)]
    tokens = jax.ShapeDtypeStruct((row_count, group_width), BF16)

    attention_flops = 2 * row_count * row_count * group_width
    head = pl.BlockSpec((row_count, HD), lambda h: (0, h))
    square = pl.BlockSpec((1, row_count, row_count), lambda h: (h, 0, 0))
    across = shift(w_out.T, "zh", 1)
    head_out, soft = pl.pallas_call(
        functools.partial(forward_kernel, scale),
        out_shape=(
            tokens,
            jax.ShapeDtypeStruct((local_heads, row_count, row_count), F32),
        ),
        grid=(local_heads,),
        in_specs=[head] * 3,
        out_specs=(head, square),
        compiler_params=WIDE,
        cost_estimate=cost(2 * attention_flops, 1 << 21, local_heads * row_count**2),
        name="attention_forward",
    )(queries, keys, values)
    heads_all = lax.all_gather(head_out, "zl", axis=0, axis_index_groups=[line])
    spread = spread_of(w_out.shape[1], features)
    cot_rows = dot_nt(cotangent, spread).astype(BF16)

    across, head_out, cot_rows = lax.optimization_barrier((across, head_out, cot_rows))
    blocks, heads_all = ring_gather(first_stage(w_out.T, across), "y", heads_all, 4)
    vmem = pl.BlockSpec(memory_space=pltpu.VMEM)
    smem = pl.BlockSpec(memory_space=pltpu.SMEM)

    def sums(near):
        return pl.pallas_call(
            sums_kernel,
            out_shape=jax.ShapeDtypeStruct((row_count, near.shape[1]), F32),
            in_specs=[vmem] * 2,
            out_specs=vmem,
            compiler_params=PARAMS,
            cost_estimate=cost(row_count * features * group_width * n, 4 << 20),
            name="gradient_sums",
        )(cot_rows, near)

    early = 2 * ((ny + 2) // 4) + 1
    own_near = jnp.concatenate(blocks[:early], 0)
    other_near = shift(own_near, "core", 1)
    own_sum = sums(own_near)
    other_sum = sums(other_near)
    own_far = jnp.concatenate(blocks[early:], 0)
    other_far = shift(own_far, "core", 1)

    terms_all = pl.pallas_call(
        functools.partial(terms_kernel, slots),
        out_shape=jax.ShapeDtypeStruct((n, row_count, group_width), BF16),
        in_specs=[smem] + [vmem] * 5,
        out_specs=vmem,
        compiler_params=PARAMS,
        cost_estimate=cost(2 * row_count * features * group_width * n, 8 << 20),
        name="gradient_terms",
    )(
        jnp.reshape(core, (1,)).astype(jnp.int32),
        cot_rows,
        own_sum,
        other_sum,
        own_far,
        other_far,
    )
    grad_out = lax.psum_scatter(
        terms_all, "zl", scatter_dimension=0, tiled=False, axis_index_groups=[line]
    )

    vmem = pl.BlockSpec(memory_space=pltpu.VMEM)
    branch_out = pl.pallas_call(
        functools.partial(output_kernel, slots),
        out_shape=jax.ShapeDtypeStruct((row_count, features), BF16),
        in_specs=[pl.BlockSpec(memory_space=pltpu.SMEM)] + [vmem] * 6,
        out_specs=vmem,
        compiler_params=PARAMS,
        cost_estimate=cost(2 * row_count * features * group_width * n, 8 << 20),
        name="output_projection",
    )(
        jnp.reshape(core, (1,)).astype(jnp.int32),
        heads_all,
        own_near,
        own_far,
        other_near,
        other_far,
        spread,
    )

    grads = pl.pallas_call(
        functools.partial(backward_kernel, scale),
        out_shape=(tokens, tokens, tokens),
        compiler_params=WIDE,
        cost_estimate=cost(4 * attention_flops, 1 << 21),
        name="attention_backward",
    )(queries, keys, values, soft, grad_out)
    return (branch_out, *grads)


def solution(mesh):
    fine = Mesh(mesh.devices.reshape(SIZES), (*DP, "zl"))
    tokens = P(DP, "zl")
    return jax.shard_map(
        on_device,
        mesh=fine,
        in_specs=(tokens, tokens, tokens, P(None, ("zl", *DP)), tokens),
        out_specs=(tokens, tokens, tokens, tokens),
        check_vma=False,
    )
```
